32 devices in a mesh: fsdp: 16 (over z, y, x), tp: 2 (over core).
Axes of the slice: x: 2, y: 2, z: 4, core: 2. Of those that a mesh axis runs over, the one named last changes fastest.
Arguments:
- tokens: bfloat16 [12608, 768], P(('fsdp', 'tp')), may hold values from -6 to 6
- cotangent: bfloat16 [12608, 768], P(('fsdp', 'tp')), may hold values from -6 to 6
- image_counts: int32 [16], P('fsdp'), may hold values from 1 to 4, as said below
- w_qkv: bfloat16 [3, 768, 768], P(None, 'fsdp', 'tp'), may hold values from -0.21875 to 0.21875
- b_query: float32 [768], P('tp'), may hold values from -3 to 3
- b_value: float32 [768], P('tp'), may hold values from -3 to 3
- w_out: bfloat16 [768, 768], P('tp', 'fsdp'), may hold values from -0.75 to 0.75
- b_out: float32 [768], replicated, may hold values from -3 to 3
- w_up: bfloat16 [768, 3072], P('fsdp', 'tp'), may hold values from -0.21875 to 0.21875
- b_up: float32 [3072], P('tp'), may hold values from -3 to 3
- w_down: bfloat16 [3072, 768], P('tp', 'fsdp'), may hold values from -0.15625 to 0.15625
- b_down: float32 [768], replicated, may hold values from -3 to 3
- gain_one: float32 [768], replicated, may hold values from 0.1 to 1.9
- shift_one: float32 [768], replicated, may hold values from -3 to 3
- gain_two: float32 [768], replicated, may hold values from 0.1 to 1.9
- shift_two: float32 [768], replicated, may hold values from -3 to 3
Outputs:
- block_out: bfloat16 [12608, 768], P(('fsdp', 'tp'))
- grad_tokens: float32 [12608, 768], P(('fsdp', 'tp'))
- grad_qkv: float32 [3, 768, 768], P(None, 'fsdp', 'tp')
- grad_out: float32 [768, 768], P('tp', 'fsdp')
- grad_up: float32 [768, 3072], P('fsdp', 'tp')
- grad_down: float32 [3072, 768], P('tp', 'fsdp')
- grad_b_query: float32 [768], P('tp')
- grad_b_value: float32 [768], P('tp')
- grad_b_out: float32 [768], replicated
- grad_b_up: float32 [3072], P('tp')
- grad_b_down: float32 [768], replicated
- grad_gain_one: float32 [768], replicated
- grad_shift_one: float32 [768], replicated
- grad_gain_two: float32 [768], replicated
- grad_shift_two: float32 [768], replicated
The draws below stay inside these ranges and needn't reach their ends.
Inputs may be any that keep to these rules, and one draw needn't show every extreme that they name: `image_counts`: entry f counts the live images among the 4 slots of index f of fsdp; live images come first; entry 0 equals 4.
All inputs are finite; a program needn't handle non-finite values.
Results may differ from the reference program's by a relative error of at most 0.015.
Values may be sent and summed in bfloat16 or wider, within the bound.
A program may use at most 128 MiB of HBM per device.

```python
import jax
import jax.numpy as jnp
from jax import lax

D = 768
HEADS = 12
HEAD_DIM = 64
FF = 3072
SEQ = 197
IMG_DEV = 4
TOKENS = 12608
N_FSDP = 16


def draw_image_counts(key, part):
    first = jax.random.fold_in(key, 7)
    counts = jax.random.randint(first, (N_FSDP,), IMG_DEV // 2, IMG_DEV + 1)
    return counts.at[0].set(IMG_DEV).astype(jnp.int32)


def shard_levels(own_key, shape, cuts, smallest, largest):
    def one(dim, shards_of):
        draws = jax.random.uniform(jax.random.fold_in(jax.random.fold_in(own_key, 6), dim), (shards_of,), jnp.float32, smallest / len(cuts), largest / len(cuts))
        return jnp.repeat(jnp.exp(draws), shape[dim] // shards_of).reshape((-1,) + (1,) * (len(shape) - dim - 1))

    level = one(*cuts[0])
    for cut in cuts[1:]:
        level = level * one(*cut)
    return level


def bell_draw(own_key, extent, spread, reach, cuts=(), kind=jnp.bfloat16):
    entries = jax.random.normal(own_key, extent, jnp.float32) * spread
    if len(cuts) > 0:
        entries = shard_levels(own_key, extent, cuts, -0.22, 0.18) * entries
    return jnp.clip(entries, min=-reach, max=reach).astype(kind)


def setup_inputs(seed: int = 0) -> dict:
    splits = jax.random.split(jax.random.key(seed), 17)
    tokens = bell_draw(splits[0], (TOKENS, D), 1.0, 6.0, ((0, 32),))
    cotangent = bell_draw(splits[1], (TOKENS, D), 1.0, 6.0, ((0, 32),))
    image_counts = draw_image_counts(jax.random.fold_in(splits[16], 71), 0)
    w_qkv = bell_draw(splits[3], (3, D, D), D ** -0.5, 0.21875, ((1, 16), (2, 2)))
    b_query = bell_draw(splits[4], (D,), 0.5, 3.0, ((0, 2),), jnp.float32)
    b_value = bell_draw(splits[5], (D,), 0.5, 3.0, ((0, 2),), jnp.float32)
    w_out = bell_draw(splits[6], (D, D), (D // 12) ** -0.5, 0.75, ((0, 2), (1, 16)))
    b_out = bell_draw(splits[7], (D,), 0.5, 3.0, (), jnp.float32)
    w_up = bell_draw(splits[8], (D, FF), D ** -0.5, 0.21875, ((0, 16), (1, 2)))
    b_up = bell_draw(splits[9], (FF,), 0.5, 3.0, ((0, 2),), jnp.float32)
    w_down = bell_draw(splits[10], (FF, D), (FF // 2) ** -0.5, 0.15625, ((0, 2), (1, 16)))
    b_down = bell_draw(splits[11], (D,), 0.5, 3.0, (), jnp.float32)
    gain_one = jnp.clip(1.0 + 0.18 * jax.random.normal(splits[12], (D,), jnp.float32), 0.1, 1.9)
    shift_one = bell_draw(splits[13], (D,), 0.5, 3.0, (), jnp.float32)
    gain_two = jnp.clip(1.0 + 0.18 * jax.random.normal(splits[14], (D,), jnp.float32), 0.1, 1.9)
    shift_two = bell_draw(splits[15], (D,), 0.5, 3.0, (), jnp.float32)
    return dict(tokens=tokens, cotangent=cotangent, image_counts=image_counts, w_qkv=w_qkv, b_query=b_query, b_value=b_value, w_out=w_out, b_out=b_out, w_up=w_up, b_up=b_up, w_down=w_down, b_down=b_down, gain_one=gain_one, shift_one=shift_one, gain_two=gain_two, shift_two=shift_two)


EPS = 1e-06
INV_ROOT_TWO = 0.7071067811865476
INV_ROOT_TWO_PI = 0.3989422804014327

def layer_norm(values, gain, shift):
    center = values - lax.optimization_barrier(jnp.mean(values, axis=-1, keepdims=True))
    scale_inv = lax.rsqrt(lax.optimization_barrier(jnp.mean(center * center, axis=-1, keepdims=True)) + EPS)
    normal = center * scale_inv
    return (normal, scale_inv, normal * gain + shift)

def norm_back(incoming, normal, scale_inv, gain):
    scaled = incoming * gain
    return scale_inv * (scaled - lax.optimization_barrier(jnp.mean(scaled, axis=-1, keepdims=True)) - normal * lax.optimization_barrier(jnp.mean(scaled * normal, axis=-1, keepdims=True)))

def gelu_parts(pre):
    cdf = 0.5 * (1.0 + lax.erf(pre * INV_ROOT_TWO))
    dens = jnp.exp(-0.5 * pre * pre) * INV_ROOT_TWO_PI
    return (pre * cdf, cdf + pre * dens)

def score_of(query, key):
    return jnp.einsum('bqhe,bkhe->bhqk', query.astype(jnp.float32), key.astype(jnp.float32)) * HEAD_DIM ** (-0.5)

def attend(query, key, value):
    scores = score_of(query, key)
    peak = lax.optimization_barrier(jnp.max(scores, axis=-1, keepdims=True))
    lse = peak + jnp.log(lax.optimization_barrier(jnp.sum(jnp.exp(scores - peak), axis=-1, keepdims=True)))
    probs = jnp.exp(scores - lse).astype(jnp.bfloat16)
    attended = jnp.einsum('bhqk,bkhe->bqhe', probs.astype(jnp.float32), value.astype(jnp.float32))
    return (attended.astype(jnp.bfloat16), lse)

def attend_back(query, key, value, lse, attended, dattended):
    scale = HEAD_DIM ** (-0.5)
    delta = lax.optimization_barrier(jnp.sum(dattended.astype(jnp.float32) * attended.astype(jnp.float32), axis=-1))
    delta = jnp.transpose(delta, (0, 2, 1))[..., None]
    probs_f = jnp.exp(score_of(query, key) - lse)
    probs = probs_f.astype(jnp.bfloat16)
    dvalue = jnp.einsum('bhqk,bqhe->bkhe', probs.astype(jnp.float32), dattended.astype(jnp.float32))
    dprobs = jnp.einsum('bqhe,bkhe->bhqk', dattended.astype(jnp.float32), value.astype(jnp.float32))
    dscores = (probs_f * (dprobs - delta)).astype(jnp.bfloat16).astype(jnp.float32)
    dquery = jnp.einsum('bhqk,bkhe->bqhe', dscores, key.astype(jnp.float32)) * scale
    dkey = jnp.einsum('bhqk,bqhe->bkhe', dscores, query.astype(jnp.float32)) * scale
    return (dquery, dkey, dvalue)

def dotf(a, b):
    return jnp.dot(a, b, preferred_element_type=jnp.float32)

def group_pass(tokens, cotangent, count, w_qkv, b_query, b_value, w_out, b_out, w_up, b_up, w_down, b_down, gain_one, shift_one, gain_two, shift_two):
    rows = tokens.shape[0]
    images = rows // SEQ
    line = jnp.arange(rows, dtype=jnp.int32) // SEQ
    live = (line < count).astype(jnp.float32)[:, None]
    shape4 = (images, SEQ, HEADS, HEAD_DIM)
    xf = tokens.astype(jnp.float32)
    xh1, rs1, n1 = layer_norm(xf, gain_one, shift_one)
    h1 = n1.astype(jnp.bfloat16)
    query = (dotf(h1, w_qkv[0]) + b_query).astype(jnp.bfloat16)
    key = dotf(h1, w_qkv[1]).astype(jnp.bfloat16)
    value = (dotf(h1, w_qkv[2]) + b_value).astype(jnp.bfloat16)
    q4, k4, v4 = (query.reshape(shape4), key.reshape(shape4), value.reshape(shape4))
    att4, lse = attend(q4, k4, v4)
    attended = att4.reshape(rows, D)
    mid = xf + dotf(attended, w_out) + b_out
    xh2, rs2, n2 = layer_norm(mid, gain_two, shift_two)
    h2 = n2.astype(jnp.bfloat16)
    pre = dotf(h2, w_up) + b_up
    gel, slope = gelu_parts(pre)
    act = gel.astype(jnp.bfloat16)
    block_out = ((mid + dotf(act, w_down) + b_down) * live).astype(jnp.bfloat16)
    dout = (cotangent.astype(jnp.float32) * live).astype(jnp.bfloat16)
    doutf = dout.astype(jnp.float32)
    g_down = dotf(act.T, dout)
    g_bdown = lax.optimization_barrier(jnp.sum(doutf, axis=0))
    dpre = dotf(dout, w_down.T) * slope
    g_bup = lax.optimization_barrier(jnp.sum(dpre, axis=0))
    dpre_b = dpre.astype(jnp.bfloat16)
    g_up = dotf(h2.T, dpre_b)
    dn2 = dotf(dpre_b, w_up.T)
    g_gain2 = lax.optimization_barrier(jnp.sum(dn2 * xh2, axis=0))
    g_shift2 = lax.optimization_barrier(jnp.sum(dn2, axis=0))
    dmid = doutf + norm_back(dn2, xh2, rs2, gain_two)
    g_bout = lax.optimization_barrier(jnp.sum(dmid, axis=0))
    dmid_b = dmid.astype(jnp.bfloat16)
    g_out = dotf(attended.T, dmid_b)
    datt = dotf(dmid_b, w_out.T).astype(jnp.bfloat16)
    dq4, dk4, dv4 = attend_back(q4, k4, v4, lse, att4, datt.reshape(shape4))
    dquery, dkey, dvalue = (dq4.reshape(rows, D), dk4.reshape(rows, D), dv4.reshape(rows, D))
    g_bq = lax.optimization_barrier(jnp.sum(dquery, axis=0))
    g_bv = lax.optimization_barrier(jnp.sum(dvalue, axis=0))
    parts = [dquery.astype(jnp.bfloat16), dkey.astype(jnp.bfloat16), dvalue.astype(jnp.bfloat16)]
    g_qkv = jnp.stack([dotf(h1.T, parts[j]) for j in range(3)])
    dn1 = dotf(parts[0], w_qkv[0].T) + dotf(parts[1], w_qkv[1].T) + dotf(parts[2], w_qkv[2].T)
    g_gain1 = lax.optimization_barrier(jnp.sum(dn1 * xh1, axis=0))
    g_shift1 = lax.optimization_barrier(jnp.sum(dn1, axis=0))
    grad_tokens = dmid + norm_back(dn1, xh1, rs1, gain_one)
    grads = (g_qkv, g_out, g_up, g_down, g_bq, g_bv, g_bout, g_bup, g_bdown, g_gain1, g_shift1, g_gain2, g_shift2)
    return (block_out, grad_tokens, grads)

def reference(tokens, cotangent, image_counts, w_qkv, b_query, b_value, w_out, b_out, w_up, b_up, w_down, b_down, gain_one, shift_one, gain_two, shift_two):
    group_rows = IMG_DEV * SEQ
    xs = tokens.reshape(N_FSDP, group_rows, D)
    cs = cotangent.reshape(N_FSDP, group_rows, D)
    zero = (jnp.zeros((3, D, D), jnp.float32), jnp.zeros((D, D), jnp.float32), jnp.zeros((D, FF), jnp.float32), jnp.zeros((FF, D), jnp.float32), jnp.zeros((D,), jnp.float32), jnp.zeros((D,), jnp.float32), jnp.zeros((D,), jnp.float32), jnp.zeros((FF,), jnp.float32), jnp.zeros((D,), jnp.float32), jnp.zeros((D,), jnp.float32), jnp.zeros((D,), jnp.float32), jnp.zeros((D,), jnp.float32), jnp.zeros((D,), jnp.float32))

    def step(carry, item):
        xg, cg, count = item
        out_g, dx_g, grads = group_pass(xg, cg, count, w_qkv, b_query, b_value, w_out, b_out, w_up, b_up, w_down, b_down, gain_one, shift_one, gain_two, shift_two)
        return (jax.tree.map(lambda a, b: a + b, carry, grads), (out_g, dx_g))
    totals, (outs, dxs) = lax.scan(step, zero, (xs, cs, image_counts))
    return (outs.reshape(TOKENS, D), dxs.reshape(TOKENS, D)) + tuple(totals)
```

```python
import jax
import jax.numpy as jnp
from jax import lax
from jax.sharding import PartitionSpec as P

HEAD_DIM = 64
SEQ = 197


EPS = 1e-06
INV_ROOT_TWO = 0.7071067811865476
INV_ROOT_TWO_PI = 0.3989422804014327
BF = jnp.bfloat16
F32 = jnp.float32


def layer_norm(values, gain, shift):
    center = values - jnp.mean(values, axis=-1, keepdims=True)
    scale_inv = lax.rsqrt(jnp.mean(center * center, axis=-1, keepdims=True) + EPS)
    normal = center * scale_inv
    return (normal, scale_inv, normal * gain + shift)


def norm_back(incoming, normal, scale_inv, gain):
    scaled = incoming * gain
    return scale_inv * (
        scaled
        - jnp.mean(scaled, axis=-1, keepdims=True)
        - normal * jnp.mean(scaled * normal, axis=-1, keepdims=True)
    )


def gelu_parts(pre):
    cdf = 0.5 * (1.0 + lax.erf(pre * INV_ROOT_TWO))
    dens = jnp.exp(-0.5 * pre * pre) * INV_ROOT_TWO_PI
    return (pre * cdf, cdf + pre * dens)


def dot_nn(left, right):
    return lax.dot_general(left, right, (((1,), (0,)), ((), ())), preferred_element_type=F32)


def dot_nt(left, right):
    return lax.dot_general(left, right, (((1,), (1,)), ((), ())), preferred_element_type=F32)


def dot_tn(left, right):
    return lax.dot_general(left, right, (((0,), (0,)), ((), ())), preferred_element_type=F32)


def score_of(query, key):
    return jnp.einsum("bqhe,bkhe->bhqk", query, key, preferred_element_type=F32) * HEAD_DIM ** (-0.5)


def attend(query, key, value):
    scores = score_of(query, key)
    peak = jnp.max(scores, axis=-1, keepdims=True)
    lse = peak + jnp.log(jnp.sum(jnp.exp(scores - peak), axis=-1, keepdims=True))
    probs = jnp.exp(scores - lse).astype(BF)
    attended = jnp.einsum("bhqk,bkhe->bqhe", probs, value, preferred_element_type=F32)
    return (attended.astype(BF), lse)


def attend_back(query, key, value, lse, attended, dattended):
    scale = HEAD_DIM ** (-0.5)
    delta = jnp.sum(dattended.astype(F32) * attended.astype(F32), axis=-1)
    delta = jnp.transpose(delta, (0, 2, 1))[..., None]
    probs_f = jnp.exp(score_of(query, key) - lse)
    probs = probs_f.astype(BF)
    dvalue = jnp.einsum("bhqk,bqhe->bkhe", probs, dattended, preferred_element_type=F32)
    dprobs = jnp.einsum("bqhe,bkhe->bhqk", dattended, value, preferred_element_type=F32)
    dscores = (probs_f * (dprobs - delta)).astype(BF)
    dquery = jnp.einsum("bhqk,bkhe->bqhe", dscores, key, preferred_element_type=F32) * scale
    dkey = jnp.einsum("bhqk,bqhe->bkhe", dscores, query, preferred_element_type=F32) * scale
    return (dquery, dkey, dvalue)


def swap(value, axis, bit):
    size = lax.axis_size(axis)
    return lax.ppermute(value, axis, [(i, i ^ (1 << bit)) for i in range(size)])


def bits_of(axis):
    return lax.axis_size(axis).bit_length() - 1


def by_bits(shard_rows):
    size = lax.axis_size("fsdp")
    return size & (size - 1) == 0 and shard_rows % 16 == 0


def my_bit(bit):
    return (lax.axis_index("fsdp") >> bit) & 1


def order_of(first):
    count = bits_of("fsdp")
    rest = [b for b in range(count) if b not in first]
    return [b for b in first if b < count] + rest


def gather(shard, first):
    if not by_bits(shard.shape[0]):
        return lax.all_gather(shard, "fsdp", axis=0, tiled=True)
    count = bits_of("fsdp")
    held = shard.reshape((1,) * count + shard.shape)
    for bit in reversed(order_of(first)):
        other = swap(held, "fsdp", bit)
        dim = count - 1 - bit
        held = jnp.where(
            my_bit(bit) == 0,
            jnp.concatenate([held, other], axis=dim),
            jnp.concatenate([other, held], axis=dim),
        )
    return held.reshape((-1, shard.shape[1]))


def scatter(own, other, first):
    size = lax.axis_size("fsdp")
    rows = own.shape[0] // size
    total = own + swap(other.astype(BF), "tp", 0).astype(F32)
    if not by_bits(rows):
        return lax.psum_scatter(total, "fsdp", scatter_dimension=0, tiled=True)
    count = bits_of("fsdp")
    total = total.reshape((2,) * count + (rows, own.shape[1]))
    for bit in order_of(first):
        dim = count - 1 - bit
        mine = my_bit(bit)
        sent = lax.dynamic_index_in_dim(total, 1 - mine, dim).astype(BF)
        kept = lax.dynamic_index_in_dim(total, mine, dim)
        total = kept + swap(sent, "fsdp", bit).astype(F32)
    return total.reshape((rows, own.shape[1]))


def all_sum(split_own, split_other, whole):
    mine = jnp.concatenate(split_own + whole)
    total = mine + swap(jnp.concatenate(split_other + whole), "tp", 0)
    size = lax.axis_size("fsdp")
    if size & (size - 1) == 0:
        for bit in range(bits_of("fsdp")):
            total = total + swap(total, "fsdp", bit)
    else:
        total = lax.psum(total, "fsdp")
    parts, at = [], 0
    for piece in split_own + whole:
        parts.append(total[at : at + piece.shape[0]])
        at += piece.shape[0]
    return parts


def local(
    tokens,
    cotangent,
    image_counts,
    w_qkv,
    b_query,
    b_value,
    w_out,
    b_out,
    w_up,
    b_up,
    w_down,
    b_down,
    gain_one,
    shift_one,
    gain_two,
    shift_two,
):
    rows, width = tokens.shape
    images = rows // SEQ
    slot = lax.axis_index("tp")
    line = (slot * rows + jnp.arange(rows, dtype=jnp.int32)) // SEQ
    live = (line < image_counts[0]).astype(F32)[:, None]
    head_width = w_qkv.shape[2]
    hidden = w_up.shape[1]
    heads = head_width // HEAD_DIM

    shard_qkv = jnp.concatenate([w_qkv[0], w_qkv[1], w_qkv[2]], axis=1)
    qkv_own = gather(shard_qkv, (0, 1))
    qkv_oth = swap(qkv_own, "tp", 0)
    mix_own = gather(jnp.concatenate([w_out.T, w_up], axis=1), (1, 0))
    mix_oth = swap(mix_own, "tp", 0)
    wd_own = gather(w_down.T, (2, 0))
    wd_oth = swap(wd_own, "tp", 0)
    wo_own, wu_own = mix_own[:, :head_width], mix_own[:, head_width:]
    wo_oth, wu_oth = mix_oth[:, :head_width], mix_oth[:, head_width:]

    bias_own = jnp.concatenate([b_query, jnp.zeros_like(b_query), b_value, b_up])
    bias_oth = swap(bias_own, "tp", 0)
    cut = 3 * head_width

    xf = tokens.astype(F32)
    xh1, rs1, n1 = layer_norm(xf, gain_one, shift_one)
    h1 = n1.astype(BF)
    shape5 = (images, SEQ, 3, heads, HEAD_DIM)
    p_own = (dot_nn(h1, qkv_own) + bias_own[:cut]).astype(BF).reshape(shape5)
    p_oth = (dot_nn(h1, qkv_oth) + bias_oth[:cut]).astype(BF).reshape(shape5)
    q4, k4, v4 = [jnp.concatenate([p_own[:, :, j], p_oth[:, :, j]], axis=2) for j in range(3)]
    att4, lse = attend(q4, k4, v4)
    att_own = att4[:, :, :heads].reshape(rows, head_width)
    att_oth = att4[:, :, heads:].reshape(rows, head_width)
    mid = xf + (dot_nt(att_own, wo_own) + dot_nt(att_oth, wo_oth)) + b_out
    xh2, rs2, n2 = layer_norm(mid, gain_two, shift_two)
    h2 = n2.astype(BF)
    gel_own, slope_own = gelu_parts(dot_nn(h2, wu_own) + bias_own[cut:])
    gel_oth, slope_oth = gelu_parts(dot_nn(h2, wu_oth) + bias_oth[cut:])
    act_own, act_oth = gel_own.astype(BF), gel_oth.astype(BF)
    block_out = ((mid + (dot_nt(act_own, wd_own) + dot_nt(act_oth, wd_oth)) + b_down) * live).astype(BF)

    dout = (cotangent.astype(F32) * live).astype(BF)
    doutf = dout.astype(F32)
    s_down = scatter(dot_tn(dout, act_own), dot_tn(dout, act_oth), (2, 0))
    dpre_own = dot_nn(dout, wd_own) * slope_own
    dpre_oth = dot_nn(dout, wd_oth) * slope_oth
    dpo, dpt = dpre_own.astype(BF), dpre_oth.astype(BF)
    s_up = scatter(dot_tn(h2, dpo), dot_tn(h2, dpt), (1, 0))
    dn2 = dot_nt(dpo, wu_own) + dot_nt(dpt, wu_oth)
    dmid = doutf + norm_back(dn2, xh2, rs2, gain_two)
    dmid_b = dmid.astype(BF)
    s_out = scatter(dot_tn(dmid_b, att_own), dot_tn(dmid_b, att_oth), (0, 1))
    part_bup, sum_bdown, sum_gain2, sum_shift2, sum_bout = all_sum(
        [jnp.sum(dpre_own, axis=0)],
        [jnp.sum(dpre_oth, axis=0)],
        [jnp.sum(doutf, axis=0), jnp.sum(dn2 * xh2, axis=0), jnp.sum(dn2, axis=0), jnp.sum(dmid, axis=0)],
    )
    shape4 = (images, SEQ, heads, HEAD_DIM)
    datt = jnp.concatenate(
        [
            dot_nn(dmid_b, wo_own).astype(BF).reshape(shape4),
            dot_nn(dmid_b, wo_oth).astype(BF).reshape(shape4),
        ],
        axis=2,
    )
    dq4, dk4, dv4 = attend_back(q4, k4, v4, lse, att4, datt)
    g_bq = jnp.sum(dq4, axis=(0, 1)).reshape(2 * head_width)
    g_bv = jnp.sum(dv4, axis=(0, 1)).reshape(2 * head_width)
    d5 = jnp.stack([dq4.astype(BF), dk4.astype(BF), dv4.astype(BF)], axis=2)
    d_own = d5[:, :, :, :heads].reshape(rows, cut)
    d_oth = d5[:, :, :, heads:].reshape(rows, cut)
    s_qkv = scatter(dot_tn(h1, d_own), dot_tn(h1, d_oth), (0, 1))
    dn1 = dot_nt(d_own, qkv_own) + dot_nt(d_oth, qkv_oth)
    grad_tokens = dmid + norm_back(dn1, xh1, rs1, gain_one)
    part_bq, part_bv, sum_gain1, sum_shift1 = all_sum(
        [g_bq[:head_width], g_bv[:head_width]],
        [g_bq[head_width:], g_bv[head_width:]],
        [jnp.sum(dn1 * xh1, axis=0), jnp.sum(dn1, axis=0)],
    )
    return (
        block_out,
        grad_tokens,
        jnp.stack([s_qkv[:, j * head_width : (j + 1) * head_width] for j in range(3)]),
        s_out.T,
        s_up,
        s_down.T,
        part_bq,
        part_bv,
        sum_bout,
        part_bup,
        sum_bdown,
        sum_gain1,
        sum_shift1,
        sum_gain2,
        sum_shift2,
    )


def solution(mesh):
    return jax.shard_map(
        local,
        mesh=mesh,
        in_specs=(
            P(("fsdp", "tp"), None),
            P(("fsdp", "tp"), None),
            P("fsdp"),
            P(None, "fsdp", "tp"),
            P("tp"),
            P("tp"),
            P("tp", "fsdp"),
            P(),
            P("fsdp", "tp"),
            P("tp"),
            P("tp", "fsdp"),
            P(),
            P(),
            P(),
            P(),
            P(),
        ),
        out_specs=(
            P(("fsdp", "tp"), None),
            P(("fsdp", "tp"), None),
            P(None, "fsdp", "tp"),
            P("tp", "fsdp"),
            P("fsdp", "tp"),
            P("tp", "fsdp"),
            P("tp"),
            P("tp"),
            P(),
            P("tp"),
            P(),
            P(),
            P(),
            P(),
            P(),
        ),
        check_vma=False,
    )
```

```python
import functools

import jax
import jax.numpy as jnp
from jax import lax
from jax.experimental import pallas as pl
from jax.experimental.pallas import tpu as pltpu
from jax.sharding import PartitionSpec as P

HEAD_DIM = 64
SEQ = 197


EPS = 1e-06
INV_ROOT_TWO = 0.7071067811865476
INV_ROOT_TWO_PI = 0.3989422804014327
BF = jnp.bfloat16
F32 = jnp.float32


def layer_norm(values, gain, shift):
    center = values - jnp.mean(values, axis=-1, keepdims=True)
    scale_inv = lax.rsqrt(jnp.mean(center * center, axis=-1, keepdims=True) + EPS)
    normal = center * scale_inv
    return (normal, scale_inv, normal * gain + shift)


def norm_back(incoming, normal, scale_inv, gain):
    scaled = incoming * gain
    return scale_inv * (
        scaled
        - jnp.mean(scaled, axis=-1, keepdims=True)
        - normal * jnp.mean(scaled * normal, axis=-1, keepdims=True)
    )


def gelu_parts(pre):
    cdf = 0.5 * (1.0 + lax.erf(pre * INV_ROOT_TWO))
    dens = jnp.exp(-0.5 * pre * pre) * INV_ROOT_TWO_PI
    return (pre * cdf, cdf + pre * dens)


def dot_nn(left, right):
    return lax.dot_general(left, right, (((1,), (0,)), ((), ())), preferred_element_type=F32)


def dot_nt(left, right):
    return lax.dot_general(left, right, (((1,), (1,)), ((), ())), preferred_element_type=F32)


def dot_tn(left, right):
    return lax.dot_general(left, right, (((0,), (0,)), ((), ())), preferred_element_type=F32)


def score_of(query, key):
    return jnp.einsum("bqhe,bkhe->bhqk", query, key, preferred_element_type=F32) * HEAD_DIM ** (-0.5)


def attend(query, key, value):
    scores = score_of(query, key)
    peak = jnp.max(scores, axis=-1, keepdims=True)
    lse = peak + jnp.log(jnp.sum(jnp.exp(scores - peak), axis=-1, keepdims=True))
    probs = jnp.exp(scores - lse).astype(BF)
    attended = jnp.einsum("bhqk,bkhe->bqhe", probs, value, preferred_element_type=F32)
    return (attended.astype(BF), lse)


def attend_back(query, key, value, lse, attended, dattended):
    scale = HEAD_DIM ** (-0.5)
    delta = jnp.sum(dattended.astype(F32) * attended.astype(F32), axis=-1)
    delta = jnp.transpose(delta, (0, 2, 1))[..., None]
    probs_f = jnp.exp(score_of(query, key) - lse)
    probs = probs_f.astype(BF)
    dvalue = jnp.einsum("bhqk,bqhe->bkhe", probs, dattended, preferred_element_type=F32)
    dprobs = jnp.einsum("bqhe,bkhe->bhqk", dattended, value, preferred_element_type=F32)
    dscores = (probs_f * (dprobs - delta)).astype(BF)
    dquery = jnp.einsum("bhqk,bkhe->bqhe", dscores, key, preferred_element_type=F32) * scale
    dkey = jnp.einsum("bhqk,bqhe->bkhe", dscores, query, preferred_element_type=F32) * scale
    return (dquery, dkey, dvalue)


def swap(value, axis, bit):
    size = lax.axis_size(axis)
    return lax.ppermute(value, axis, [(i, i ^ (1 << bit)) for i in range(size)])


def bits_of(axis):
    return lax.axis_size(axis).bit_length() - 1


def by_bits(shard_rows):
    size = lax.axis_size("fsdp")
    return size & (size - 1) == 0 and shard_rows % 16 == 0


def order_of(first):
    count = bits_of("fsdp")
    rest = [b for b in range(count) if b not in first]
    return [b for b in first if b < count] + rest


def enter(count):
    me = lax.axis_index("fsdp")
    bits = [(me // (1 << b)) % 2 for b in range(count)]
    near = [{"fsdp": me + (1 - 2 * bits[b]) * (1 << b)} for b in range(count)]
    twin = {"tp": 1 - lax.axis_index("tp")}
    barrier = pltpu.get_barrier_semaphore()
    for device in near + [twin]:
        pl.semaphore_signal(barrier, inc=1, device_id=device, device_id_type=pl.DeviceIdType.MESH)
    pl.semaphore_wait(barrier, count + 1)
    return bits, near, twin


def place(bits, rel):
    return sum((1 - m if (rel >> b) & 1 else m) * (1 << b) for b, m in enumerate(bits))


def remote(src, dst, sems, at, device):
    return pltpu.make_async_remote_copy(
        src_ref=src,
        dst_ref=dst,
        send_sem=sems[0].at[at],
        recv_sem=sems[1].at[at],
        device_id=device,
        device_id_type=pl.DeviceIdType.MESH,
    )


def gather_kernel(count, steps, *refs):
    k = len(steps)
    shards, own, oth = refs[:k], refs[k : 2 * k], refs[2 * k : 3 * k]
    ring, pair, here = refs[3 * k : 3 * k + 2], refs[3 * k + 2 : 3 * k + 4], refs[3 * k + 4]
    size = 1 << count
    bits, near, twin = enter(count)
    copies = []

    def spread(c, rel, done):
        block = own[c].at[place(bits, rel)]
        src = shards[c] if rel == 0 else block
        for bit in steps[c][done:]:
            copies.append(remote(src, block, ring, c * size + (rel | 1 << bit), near[bit]))
            copies[-1].start()
        copies.append(remote(src, oth[c].at[place(bits, rel)], pair, c * size + rel, twin))
        copies[-1].start()

    keep = [pltpu.make_async_copy(shards[c], own[c].at[place(bits, 0)], here.at[c]) for c in range(k)]
    for c in range(k):
        spread(c, 0, 0)
        keep[c].start()
    held = [[0] for _ in range(k)]
    for step in range(count):
        for c in range(k):
            bit = steps[c][step]
            fresh = [rel | 1 << bit for rel in held[c]]
            for rel in fresh:
                block = own[c].at[place(bits, rel)]
                remote(block, block, ring, c * size + rel, near[bit]).wait_recv()
                spread(c, rel, step + 1)
            held[c] = held[c] + fresh
    for c in range(k):
        for rel in range(size):
            block = oth[c].at[place(bits, rel)]
            remote(block, block, pair, c * size + rel, twin).wait_recv()
        keep[c].wait()
    for copy in copies:
        copy.wait_send()


def gather_all(shards, firsts):
    if not by_bits(shards[0].shape[0]):
        own = [lax.all_gather(s, "fsdp", axis=0, tiled=True) for s in shards]
        return own, [swap(o, "tp", 0) for o in own]
    size, count, k = lax.axis_size("fsdp"), bits_of("fsdp"), len(shards)
    whole = [jax.ShapeDtypeStruct((size,) + s.shape, s.dtype) for s in shards]
    outs = pl.pallas_call(
        functools.partial(gather_kernel, count, [order_of(f)[::-1] for f in firsts]),
        out_shape=whole + whole,
        in_specs=[pl.BlockSpec(memory_space=pl.ANY)] * k,
        out_specs=[pl.BlockSpec(memory_space=pl.ANY)] * (2 * k),
        scratch_shapes=[pltpu.SemaphoreType.DMA((k * size,))] * 4 + [pltpu.SemaphoreType.DMA((k,))],
        compiler_params=pltpu.CompilerParams(collective_id=0, has_side_effects=True),
        name="gather_all",
    )(*shards)
    outs = [o.reshape((-1, o.shape[2])) for o in outs]
    return outs[:k], outs[k:]


def scatter_kernel(count, orders, *refs):
    k = len(orders)
    own, oth, out = refs[:k], refs[k : 2 * k], refs[2 * k : 3 * k]
    from_twin, sent, came = refs[3 * k : 4 * k], refs[4 * k : 5 * k], refs[5 * k : 6 * k]
    ring, pair = refs[6 * k : 6 * k + 2], refs[6 * k + 2 : 6 * k + 4]
    size = 1 << count
    bits, near, twin = enter(count)
    copies = []

    def stage(c, step):
        done = sum(1 << b for b in orders[c][:step])
        if step == count:
            return [0]
        return [r for r in range(size) if r & done == 0 and (r >> orders[c][step]) & 1]

    for step in range(count + 1):
        for c in range(k):
            for rel in stage(c, step):
                copy = remote(oth[c].at[place(bits, rel)], from_twin[c].at[rel], pair, c * size + rel, twin)
                copy.start()
                copies.append(copy)
    for step in range(count + 1):
        for c in range(k):
            for rel in stage(c, step):
                slot = from_twin[c].at[rel]
                remote(slot, slot, pair, c * size + rel, twin).wait_recv()
                total = own[c][place(bits, rel)].astype(F32) + from_twin[c][rel].astype(F32)
                for bit in orders[c][:step]:
                    at = rel | 1 << bit
                    slot = came[c].at[at]
                    remote(slot, slot, ring, c * size + at, near[bit]).wait_recv()
                    total = total + came[c][at].astype(F32)
                if step == count:
                    out[c][...] = total
                else:
                    sent[c][rel] = total.astype(BF)
                    copy = remote(
                        sent[c].at[rel], came[c].at[rel], ring, c * size + rel, near[orders[c][step]]
                    )
                    copy.start()
                    copies.append(copy)
    for copy in copies:
        copy.wait_send()


def scatter_all(owns, others, firsts):
    size = lax.axis_size("fsdp")
    rows = owns[0].shape[0] // size
    owns, others = [o.astype(BF) for o in owns], [o.astype(BF) for o in others]
    if not by_bits(rows):
        return [
            lax.psum_scatter(
                o.astype(F32) + swap(t, "tp", 0).astype(F32), "fsdp", scatter_dimension=0, tiled=True
            )
            for o, t in zip(owns, others)
        ]
    count, k = bits_of("fsdp"), len(owns)
    blocks = [(size, rows, o.shape[1]) for o in owns]
    return pl.pallas_call(
        functools.partial(scatter_kernel, count, [order_of(f) for f in firsts]),
        out_shape=[jax.ShapeDtypeStruct(b[1:], F32) for b in blocks],
        in_specs=[pl.BlockSpec(memory_space=pltpu.VMEM)] * k + [pl.BlockSpec(memory_space=pl.ANY)] * k,
        out_specs=[pl.BlockSpec(memory_space=pltpu.VMEM)] * k,
        scratch_shapes=[pltpu.VMEM(b, BF) for b in blocks] * 3
        + [pltpu.SemaphoreType.DMA((k * size,))] * 4,
        compiler_params=pltpu.CompilerParams(
            collective_id=1, has_side_effects=True, vmem_limit_bytes=48 * 1024 * 1024
        ),
        name="scatter_all",
    )(*[o.reshape(b) for o, b in zip(owns, blocks)], *[o.reshape(b) for o, b in zip(others, blocks)])


def all_sum(split_own, split_other, whole):
    mine = jnp.concatenate(split_own + whole)
    total = mine + swap(jnp.concatenate(split_other + whole), "tp", 0)
    size = lax.axis_size("fsdp")
    if size & (size - 1) == 0:
        for bit in range(bits_of("fsdp")):
            total = total + swap(total, "fsdp", bit)
    else:
        total = lax.psum(total, "fsdp")
    parts, at = [], 0
    for piece in split_own + whole:
        parts.append(total[at : at + piece.shape[0]])
        at += piece.shape[0]
    return parts


def local(
    tokens,
    cotangent,
    image_counts,
    w_qkv,
    b_query,
    b_value,
    w_out,
    b_out,
    w_up,
    b_up,
    w_down,
    b_down,
    gain_one,
    shift_one,
    gain_two,
    shift_two,
):
    rows, width = tokens.shape
    images = rows // SEQ
    slot = lax.axis_index("tp")
    line = (slot * rows + jnp.arange(rows, dtype=jnp.int32)) // SEQ
    live = (line < image_counts[0]).astype(F32)[:, None]
    head_width = w_qkv.shape[2]
    hidden = w_up.shape[1]
    heads = head_width // HEAD_DIM

    shard_qkv = jnp.concatenate([w_qkv[0], w_qkv[1], w_qkv[2]], axis=1)
    (qkv_own, mix_own, wd_own), (qkv_oth, mix_oth, wd_oth) = gather_all(
        [shard_qkv, jnp.concatenate([w_out.T, w_up], axis=1), w_down.T], [(0, 1), (1, 0), (2, 0)]
    )
    wo_own, wu_own = mix_own[:, :head_width], mix_own[:, head_width:]
    wo_oth, wu_oth = mix_oth[:, :head_width], mix_oth[:, head_width:]

    bias_own = jnp.concatenate([b_query, jnp.zeros_like(b_query), b_value, b_up])
    bias_oth = swap(bias_own, "tp", 0)
    cut = 3 * head_width

    xf = tokens.astype(F32)
    xh1, rs1, n1 = layer_norm(xf, gain_one, shift_one)
    h1 = n1.astype(BF)
    shape5 = (images, SEQ, 3, heads, HEAD_DIM)
    p_own = (dot_nn(h1, qkv_own) + bias_own[:cut]).astype(BF).reshape(shape5)
    p_oth = (dot_nn(h1, qkv_oth) + bias_oth[:cut]).astype(BF).reshape(shape5)
    q4, k4, v4 = [jnp.concatenate([p_own[:, :, j], p_oth[:, :, j]], axis=2) for j in range(3)]
    att4, lse = attend(q4, k4, v4)
    att_own = att4[:, :, :heads].reshape(rows, head_width)
    att_oth = att4[:, :, heads:].reshape(rows, head_width)
    mid = xf + (dot_nt(att_own, wo_own) + dot_nt(att_oth, wo_oth)) + b_out
    xh2, rs2, n2 = layer_norm(mid, gain_two, shift_two)
    h2 = n2.astype(BF)
    gel_own, slope_own = gelu_parts(dot_nn(h2, wu_own) + bias_own[cut:])
    gel_oth, slope_oth = gelu_parts(dot_nn(h2, wu_oth) + bias_oth[cut:])
    act_own, act_oth = gel_own.astype(BF), gel_oth.astype(BF)
    block_out = ((mid + (dot_nt(act_own, wd_own) + dot_nt(act_oth, wd_oth)) + b_down) * live).astype(BF)

    dout = (cotangent.astype(F32) * live).astype(BF)
    doutf = dout.astype(F32)
    dpre_own = dot_nn(dout, wd_own) * slope_own
    dpre_oth = dot_nn(dout, wd_oth) * slope_oth
    dpo, dpt = dpre_own.astype(BF), dpre_oth.astype(BF)
    dn2 = dot_nt(dpo, wu_own) + dot_nt(dpt, wu_oth)
    dmid = doutf + norm_back(dn2, xh2, rs2, gain_two)
    dmid_b = dmid.astype(BF)
    part_bup, sum_bdown, sum_gain2, sum_shift2, sum_bout = all_sum(
        [jnp.sum(dpre_own, axis=0)],
        [jnp.sum(dpre_oth, axis=0)],
        [jnp.sum(doutf, axis=0), jnp.sum(dn2 * xh2, axis=0), jnp.sum(dn2, axis=0), jnp.sum(dmid, axis=0)],
    )
    shape4 = (images, SEQ, heads, HEAD_DIM)
    datt = jnp.concatenate(
        [
            dot_nn(dmid_b, wo_own).astype(BF).reshape(shape4),
            dot_nn(dmid_b, wo_oth).astype(BF).reshape(shape4),
        ],
        axis=2,
    )
    dq4, dk4, dv4 = attend_back(q4, k4, v4, lse, att4, datt)
    g_bq = jnp.sum(dq4, axis=(0, 1)).reshape(2 * head_width)
    g_bv = jnp.sum(dv4, axis=(0, 1)).reshape(2 * head_width)
    d5 = jnp.stack([dq4.astype(BF), dk4.astype(BF), dv4.astype(BF)], axis=2)
    d_own = d5[:, :, :, :heads].reshape(rows, cut)
    d_oth = d5[:, :, :, heads:].reshape(rows, cut)
    dn1 = dot_nt(d_own, qkv_own) + dot_nt(d_oth, qkv_oth)
    grad_tokens = dmid + norm_back(dn1, xh1, rs1, gain_one)
    part_bq, part_bv, sum_gain1, sum_shift1 = all_sum(
        [g_bq[:head_width], g_bv[:head_width]],
        [g_bq[head_width:], g_bv[head_width:]],
        [jnp.sum(dn1 * xh1, axis=0), jnp.sum(dn1, axis=0)],
    )
    s_heads, s_up, s_down = scatter_all(
        [
            jnp.concatenate([dot_tn(h1, d_own).astype(BF), dot_tn(dmid_b, att_own).astype(BF)], axis=1),
            dot_tn(h2, dpo),
            dot_tn(dout, act_own),
        ],
        [
            jnp.concatenate([dot_tn(h1, d_oth).astype(BF), dot_tn(dmid_b, att_oth).astype(BF)], axis=1),
            dot_tn(h2, dpt),
            dot_tn(dout, act_oth),
        ],
        [(0, 1), (1, 0), (2, 0)],
    )
    s_qkv, s_out = s_heads[:, :cut], s_heads[:, cut:]
    return (
        block_out,
        grad_tokens,
        jnp.stack([s_qkv[:, j * head_width : (j + 1) * head_width] for j in range(3)]),
        s_out.T,
        s_up,
        s_down.T,
        part_bq,
        part_bv,
        sum_bout,
        part_bup,
        sum_bdown,
        sum_gain1,
        sum_shift1,
        sum_gain2,
        sum_shift2,
    )


def solution(mesh):
    return jax.shard_map(
        local,
        mesh=mesh,
        in_specs=(
            P(("fsdp", "tp"), None),
            P(("fsdp", "tp"), None),
            P("fsdp"),
            P(None, "fsdp", "tp"),
            P("tp"),
            P("tp"),
            P("tp", "fsdp"),
            P(),
            P("fsdp", "tp"),
            P("tp"),
            P("tp", "fsdp"),
            P(),
            P(),
            P(),
            P(),
            P(),
        ),
        out_specs=(
            P(("fsdp", "tp"), None),
            P(("fsdp", "tp"), None),
            P(None, "fsdp", "tp"),
            P("tp", "fsdp"),
            P("fsdp", "tp"),
            P("tp", "fsdp"),
            P("tp"),
            P("tp"),
            P(),
            P("tp"),
            P(),
            P(),
            P(),
            P(),
            P(),
        ),
        check_vma=False,
    )
```

```python
import functools

import jax
import jax.numpy as jnp
from jax import lax
from jax.experimental import pallas as pl
from jax.experimental.pallas import tpu as pltpu
from jax.sharding import PartitionSpec as P

HEAD_DIM = 64
SEQ = 197


EPS = 1e-06
INV_ROOT_TWO = 0.7071067811865476
INV_ROOT_TWO_PI = 0.3989422804014327
BF = jnp.bfloat16
F32 = jnp.float32


def layer_norm(values, gain, shift):
    center = values - jnp.mean(values, axis=-1, keepdims=True)
    scale_inv = lax.rsqrt(jnp.mean(center * center, axis=-1, keepdims=True) + EPS)
    normal = center * scale_inv
    return (normal, scale_inv, normal * gain + shift)


def norm_back(incoming, normal, scale_inv, gain):
    scaled = incoming * gain
    return scale_inv * (
        scaled
        - jnp.mean(scaled, axis=-1, keepdims=True)
        - normal * jnp.mean(scaled * normal, axis=-1, keepdims=True)
    )


def gelu_parts(pre):
    cdf = 0.5 * (1.0 + lax.erf(pre * INV_ROOT_TWO))
    dens = jnp.exp(-0.5 * pre * pre) * INV_ROOT_TWO_PI
    return (pre * cdf, cdf + pre * dens)


def dot_nn(left, right):
    return lax.dot_general(left, right, (((1,), (0,)), ((), ())), preferred_element_type=F32)


def dot_nt(left, right):
    return lax.dot_general(left, right, (((1,), (1,)), ((), ())), preferred_element_type=F32)


def dot_tn(left, right):
    return lax.dot_general(left, right, (((0,), (0,)), ((), ())), preferred_element_type=F32)


def score_of(query, key):
    return jnp.einsum("bqhe,bkhe->bhqk", query, key, preferred_element_type=F32) * HEAD_DIM ** (-0.5)


def attend(query, key, value):
    scores = score_of(query, key)
    peak = jnp.max(scores, axis=-1, keepdims=True)
    lse = peak + jnp.log(jnp.sum(jnp.exp(scores - peak), axis=-1, keepdims=True))
    probs = jnp.exp(scores - lse).astype(BF)
    attended = jnp.einsum("bhqk,bkhe->bqhe", probs, value, preferred_element_type=F32)
    return (attended.astype(BF), lse)


def attend_back(query, key, value, lse, attended, dattended):
    scale = HEAD_DIM ** (-0.5)
    delta = jnp.sum(dattended.astype(F32) * attended.astype(F32), axis=-1)
    delta = jnp.transpose(delta, (0, 2, 1))[..., None]
    probs_f = jnp.exp(score_of(query, key) - lse)
    probs = probs_f.astype(BF)
    dvalue = jnp.einsum("bhqk,bqhe->bkhe", probs, dattended, preferred_element_type=F32)
    dprobs = jnp.einsum("bqhe,bkhe->bhqk", dattended, value, preferred_element_type=F32)
    dscores = (probs_f * (dprobs - delta)).astype(BF)
    dquery = jnp.einsum("bhqk,bkhe->bqhe", dscores, key, preferred_element_type=F32) * scale
    dkey = jnp.einsum("bhqk,bqhe->bkhe", dscores, query, preferred_element_type=F32) * scale
    return (dquery, dkey, dvalue)


def swap(value, axis, bit):
    size = lax.axis_size(axis)
    return lax.ppermute(value, axis, [(i, i ^ (1 << bit)) for i in range(size)])


def bits_of(axis):
    return lax.axis_size(axis).bit_length() - 1


def by_bits(shard_rows):
    size = lax.axis_size("fsdp")
    return size & (size - 1) == 0 and shard_rows % 16 == 0


def order_of(first):
    count = bits_of("fsdp")
    rest = [b for b in range(count) if b not in first]
    return [b for b in first if b < count] + rest


def enter(count):
    me = lax.axis_index("fsdp")
    bits = [(me // (1 << b)) % 2 for b in range(count)]
    near = [{"fsdp": me + (1 - 2 * bits[b]) * (1 << b)} for b in range(count)]
    twin = {"tp": 1 - lax.axis_index("tp")}
    barrier = pltpu.get_barrier_semaphore()
    for device in near + [twin]:
        pl.semaphore_signal(barrier, inc=1, device_id=device, device_id_type=pl.DeviceIdType.MESH)
    pl.semaphore_wait(barrier, count + 1)
    return bits, near, twin


def place(bits, rel):
    return sum((1 - m if (rel >> b) & 1 else m) * (1 << b) for b, m in enumerate(bits))


def remote(src, dst, sems, at, device):
    return pltpu.make_async_remote_copy(
        src_ref=src,
        dst_ref=dst,
        send_sem=sems[0].at[at],
        recv_sem=sems[1].at[at],
        device_id=device,
        device_id_type=pl.DeviceIdType.MESH,
    )


def gather_kernel(count, steps, *refs):
    k = len(steps)
    shards, own, oth = refs[:k], refs[k : 2 * k], refs[2 * k : 3 * k]
    ring, pair, here = refs[3 * k : 3 * k + 2], refs[3 * k + 2 : 3 * k + 4], refs[3 * k + 4]
    size = 1 << count
    bits, near, twin = enter(count)
    copies = []

    def spread(c, rel, done):
        block = own[c].at[place(bits, rel)]
        src = shards[c] if rel == 0 else block
        for bit in steps[c][done:]:
            copies.append(remote(src, block, ring, c * size + (rel | 1 << bit), near[bit]))
            copies[-1].start()
        copies.append(remote(src, oth[c].at[place(bits, rel)], pair, c * size + rel, twin))
        copies[-1].start()

    keep = [pltpu.make_async_copy(shards[c], own[c].at[place(bits, 0)], here.at[c]) for c in range(k)]
    for c in range(k):
        spread(c, 0, 0)
        keep[c].start()
    held = [[0] for _ in range(k)]
    for step in range(count):
        for c in range(k):
            bit = steps[c][step]
            fresh = [rel | 1 << bit for rel in held[c]]
            for rel in fresh:
                block = own[c].at[place(bits, rel)]
                remote(block, block, ring, c * size + rel, near[bit]).wait_recv()
                spread(c, rel, step + 1)
            held[c] = held[c] + fresh
    for c in range(k):
        for rel in range(size):
            block = oth[c].at[place(bits, rel)]
            remote(block, block, pair, c * size + rel, twin).wait_recv()
        keep[c].wait()
    for copy in copies:
        copy.wait_send()


def gather_all(shards, firsts):
    if not by_bits(shards[0].shape[0]):
        own = [lax.all_gather(s, "fsdp", axis=0, tiled=True) for s in shards]
        return own, [swap(o, "tp", 0) for o in own]
    size, count, k = lax.axis_size("fsdp"), bits_of("fsdp"), len(shards)
    whole = [jax.ShapeDtypeStruct((size,) + s.shape, s.dtype) for s in shards]
    outs = pl.pallas_call(
        functools.partial(gather_kernel, count, [order_of(f)[::-1] for f in firsts]),
        out_shape=whole + whole,
        in_specs=[pl.BlockSpec(memory_space=pl.ANY)] * k,
        out_specs=[pl.BlockSpec(memory_space=pl.ANY)] * (2 * k),
        scratch_shapes=[pltpu.SemaphoreType.DMA((k * size,))] * 4 + [pltpu.SemaphoreType.DMA((k,))],
        compiler_params=pltpu.CompilerParams(collective_id=0, has_side_effects=True),
        name="gather_all",
    )(*shards)
    outs = [o.reshape((-1, o.shape[2])) for o in outs]
    return outs[:k], outs[k:]


def scatter_kernel(count, orders, *refs):
    k = len(orders)
    own, oth, refs = refs[:k], refs[k : 2 * k], refs[2 * k :]
    vec_own, vec_oth, refs = refs[0], refs[1], refs[2:]
    out, vec_out, refs = refs[:k], refs[k], refs[k + 1 :]
    from_twin, sent, came, refs = refs[:k], refs[k : 2 * k], refs[2 * k : 3 * k], refs[3 * k :]
    vec_sent, vec_came, ring, pair, line = refs[0], refs[1], refs[2:4], refs[4:6], refs[6:8]
    size = 1 << count
    bits, near, twin = enter(count)
    copies = []

    def stage(c, step):
        done = sum(1 << b for b in orders[c][:step])
        if step == count:
            return [0]
        return [r for r in range(size) if r & done == 0 and (r >> orders[c][step]) & 1]

    copies.append(remote(vec_oth, vec_came.at[0], line, 0, twin))
    copies[0].start()
    for step in range(count + 1):
        for c in range(k):
            for rel in stage(c, step):
                copy = remote(oth[c].at[place(bits, rel)], from_twin[c].at[rel], pair, c * size + rel, twin)
                copy.start()
                copies.append(copy)
    vector = vec_own[...]
    for step in range(count + 1):
        slot = vec_came.at[step]
        remote(slot, slot, line, step, twin).wait_recv()
        vector = vector + vec_came[step]
        if step == count:
            vec_out[...] = vector
        else:
            vec_sent[step] = vector
            copy = remote(vec_sent.at[step], vec_came.at[step + 1], line, step + 1, near[step])
            copy.start()
            copies.append(copy)
        for c in range(k):
            for rel in stage(c, step):
                slot = from_twin[c].at[rel]
                remote(slot, slot, pair, c * size + rel, twin).wait_recv()
                total = own[c][place(bits, rel)].astype(F32) + from_twin[c][rel].astype(F32)
                for bit in orders[c][:step]:
                    at = rel | 1 << bit
                    slot = came[c].at[at]
                    remote(slot, slot, ring, c * size + at, near[bit]).wait_recv()
                    total = total + came[c][at].astype(F32)
                if step == count:
                    out[c][...] = total
                else:
                    sent[c][rel] = total.astype(BF)
                    copy = remote(
                        sent[c].at[rel], came[c].at[rel], ring, c * size + rel, near[orders[c][step]]
                    )
                    copy.start()
                    copies.append(copy)
    for copy in copies:
        copy.wait_send()


def scatter_all(owns, others, firsts, split_own, split_other, whole):
    size = lax.axis_size("fsdp")
    rows = owns[0].shape[0] // size
    owns, others = [o.astype(BF) for o in owns], [o.astype(BF) for o in others]
    if not by_bits(rows):
        return [
            lax.psum_scatter(
                o.astype(F32) + swap(t, "tp", 0).astype(F32), "fsdp", scatter_dimension=0, tiled=True
            )
            for o, t in zip(owns, others)
        ], all_sum(split_own, split_other, whole)
    count, k = bits_of("fsdp"), len(owns)
    blocks = [(size, rows, o.shape[1]) for o in owns]
    vec_own, vec_oth = jnp.concatenate(split_own + whole), jnp.concatenate(split_other + whole)
    length = vec_own.shape[0]
    lines = -(-length // 1024) * 8
    vec_own, vec_oth = [
        jnp.pad(v, (0, lines * 128 - length)).reshape(lines, 128) for v in (vec_own, vec_oth)
    ]
    in_vmem = pl.BlockSpec(memory_space=pltpu.VMEM)
    *sums, total = pl.pallas_call(
        functools.partial(scatter_kernel, count, [order_of(f) for f in firsts]),
        out_shape=[jax.ShapeDtypeStruct(b[1:], F32) for b in blocks]
        + [jax.ShapeDtypeStruct((lines, 128), F32)],
        in_specs=[in_vmem] * k + [pl.BlockSpec(memory_space=pl.ANY)] * k + [in_vmem] * 2,
        out_specs=[in_vmem] * (k + 1),
        scratch_shapes=[pltpu.VMEM(b, BF) for b in blocks] * 3
        + [pltpu.VMEM((count, lines, 128), F32), pltpu.VMEM((count + 1, lines, 128), F32)]
        + [pltpu.SemaphoreType.DMA((k * size,))] * 4
        + [pltpu.SemaphoreType.DMA((count + 1,))] * 2,
        compiler_params=pltpu.CompilerParams(
            collective_id=1, has_side_effects=True, vmem_limit_bytes=48 * 1024 * 1024
        ),
        name="scatter_all",
    )(*[o.reshape(b) for o, b in zip(owns, blocks)], *[o.reshape(b) for o, b in zip(others, blocks)], vec_own, vec_oth)
    return sums, cut_up(total.reshape(-1), split_own + whole)


def all_sum(split_own, split_other, whole):
    mine = jnp.concatenate(split_own + whole)
    total = mine + swap(jnp.concatenate(split_other + whole), "tp", 0)
    size = lax.axis_size("fsdp")
    if size & (size - 1) == 0:
        for bit in range(bits_of("fsdp")):
            total = total + swap(total, "fsdp", bit)
    else:
        total = lax.psum(total, "fsdp")
    return cut_up(total, split_own + whole)


def cut_up(total, pieces):
    parts, at = [], 0
    for piece in pieces:
        parts.append(total[at : at + piece.shape[0]])
        at += piece.shape[0]
    return parts


def local(
    tokens,
    cotangent,
    image_counts,
    w_qkv,
    b_query,
    b_value,
    w_out,
    b_out,
    w_up,
    b_up,
    w_down,
    b_down,
    gain_one,
    shift_one,
    gain_two,
    shift_two,
):
    rows, width = tokens.shape
    images = rows // SEQ
    slot = lax.axis_index("tp")
    line = (slot * rows + jnp.arange(rows, dtype=jnp.int32)) // SEQ
    live = (line < image_counts[0]).astype(F32)[:, None]
    head_width = w_qkv.shape[2]
    hidden = w_up.shape[1]
    heads = head_width // HEAD_DIM

    shard_qkv = jnp.concatenate([w_qkv[0], w_qkv[1], w_qkv[2]], axis=1)
    (qkv_own, mix_own, wd_own), (qkv_oth, mix_oth, wd_oth) = gather_all(
        [shard_qkv, jnp.concatenate([w_out.T, w_up], axis=1), w_down.T], [(0, 1), (1, 0), (2, 0)]
    )
    wo_own, wu_own = mix_own[:, :head_width], mix_own[:, head_width:]
    wo_oth, wu_oth = mix_oth[:, :head_width], mix_oth[:, head_width:]

    bias_own = jnp.concatenate([b_query, jnp.zeros_like(b_query), b_value, b_up])
    bias_oth = swap(bias_own, "tp", 0)
    cut = 3 * head_width

    xf = tokens.astype(F32)
    xh1, rs1, n1 = layer_norm(xf, gain_one, shift_one)
    h1 = n1.astype(BF)
    shape5 = (images, SEQ, 3, heads, HEAD_DIM)
    p_own = (dot_nn(h1, qkv_own) + bias_own[:cut]).astype(BF).reshape(shape5)
    p_oth = (dot_nn(h1, qkv_oth) + bias_oth[:cut]).astype(BF).reshape(shape5)
    q4, k4, v4 = [jnp.concatenate([p_own[:, :, j], p_oth[:, :, j]], axis=2) for j in range(3)]
    att4, lse = attend(q4, k4, v4)
    att_own = att4[:, :, :heads].reshape(rows, head_width)
    att_oth = att4[:, :, heads:].reshape(rows, head_width)
    mid = xf + (dot_nt(att_own, wo_own) + dot_nt(att_oth, wo_oth)) + b_out
    xh2, rs2, n2 = layer_norm(mid, gain_two, shift_two)
    h2 = n2.astype(BF)
    gel_own, slope_own = gelu_parts(dot_nn(h2, wu_own) + bias_own[cut:])
    gel_oth, slope_oth = gelu_parts(dot_nn(h2, wu_oth) + bias_oth[cut:])
    act_own, act_oth = gel_own.astype(BF), gel_oth.astype(BF)
    block_out = ((mid + (dot_nt(act_own, wd_own) + dot_nt(act_oth, wd_oth)) + b_down) * live).astype(BF)

    dout = (cotangent.astype(F32) * live).astype(BF)
    doutf = dout.astype(F32)
    dpre_own = dot_nn(dout, wd_own) * slope_own
    dpre_oth = dot_nn(dout, wd_oth) * slope_oth
    dpo, dpt = dpre_own.astype(BF), dpre_oth.astype(BF)
    dn2 = dot_nt(dpo, wu_own) + dot_nt(dpt, wu_oth)
    dmid = doutf + norm_back(dn2, xh2, rs2, gain_two)
    dmid_b = dmid.astype(BF)
    shape4 = (images, SEQ, heads, HEAD_DIM)
    datt = jnp.concatenate(
        [
            dot_nn(dmid_b, wo_own).astype(BF).reshape(shape4),
            dot_nn(dmid_b, wo_oth).astype(BF).reshape(shape4),
        ],
        axis=2,
    )
    dq4, dk4, dv4 = attend_back(q4, k4, v4, lse, att4, datt)
    g_bq = jnp.sum(dq4, axis=(0, 1)).reshape(2 * head_width)
    g_bv = jnp.sum(dv4, axis=(0, 1)).reshape(2 * head_width)
    d5 = jnp.stack([dq4.astype(BF), dk4.astype(BF), dv4.astype(BF)], axis=2)
    d_own = d5[:, :, :, :heads].reshape(rows, cut)
    d_oth = d5[:, :, :, heads:].reshape(rows, cut)
    dn1 = dot_nt(d_own, qkv_own) + dot_nt(d_oth, qkv_oth)
    grad_tokens = dmid + norm_back(dn1, xh1, rs1, gain_one)
    (s_heads, s_up, s_down), vectors = scatter_all(
        [
            jnp.concatenate([dot_tn(h1, d_own).astype(BF), dot_tn(dmid_b, att_own).astype(BF)], axis=1),
            dot_tn(h2, dpo),
            dot_tn(dout, act_own),
        ],
        [
            jnp.concatenate([dot_tn(h1, d_oth).astype(BF), dot_tn(dmid_b, att_oth).astype(BF)], axis=1),
            dot_tn(h2, dpt),
            dot_tn(dout, act_oth),
        ],
        [(0, 1), (1, 0), (2, 0)],
        [jnp.sum(dpre_own, axis=0), g_bq[:head_width], g_bv[:head_width]],
        [jnp.sum(dpre_oth, axis=0), g_bq[head_width:], g_bv[head_width:]],
        [
            jnp.sum(doutf, axis=0),
            jnp.sum(dn2 * xh2, axis=0),
            jnp.sum(dn2, axis=0),
            jnp.sum(dmid, axis=0),
            jnp.sum(dn1 * xh1, axis=0),
            jnp.sum(dn1, axis=0),
        ],
    )
    part_bup, part_bq, part_bv, sum_bdown, sum_gain2, sum_shift2, sum_bout, sum_gain1, sum_shift1 = vectors
    s_qkv, s_out = s_heads[:, :cut], s_heads[:, cut:]
    return (
        block_out,
        grad_tokens,
        jnp.stack([s_qkv[:, j * head_width : (j + 1) * head_width] for j in range(3)]),
        s_out.T,
        s_up,
        s_down.T,
        part_bq,
        part_bv,
        sum_bout,
        part_bup,
        sum_bdown,
        sum_gain1,
        sum_shift1,
        sum_gain2,
        sum_shift2,
    )


def solution(mesh):
    return jax.shard_map(
        local,
        mesh=mesh,
        in_specs=(
            P(("fsdp", "tp"), None),
            P(("fsdp", "tp"), None),
            P("fsdp"),
            P(None, "fsdp", "tp"),
            P("tp"),
            P("tp"),
            P("tp", "fsdp"),
            P(),
            P("fsdp", "tp"),
            P("tp"),
            P("tp", "fsdp"),
            P(),
            P(),
            P(),
            P(),
            P(),
        ),
        out_specs=(
            P(("fsdp", "tp"), None),
            P(("fsdp", "tp"), None),
            P(None, "fsdp", "tp"),
            P("tp", "fsdp"),
            P("fsdp", "tp"),
            P("tp", "fsdp"),
            P("tp"),
            P("tp"),
            P(),
            P("tp"),
            P(),
            P(),
            P(),
            P(),
            P(),
        ),
        check_vma=False,
    )
```
